32 devices in a mesh: slab: 2 (over x), ex: 16 (over z, y, core).
Axes of the slice: x: 2, y: 2, z: 4, core: 2. Of those that a mesh axis runs over, the one named last changes fastest.
Arguments:
- train_grads: bfloat16 [16384, 12, 256], P(('slab', 'ex')), parts along dimension 0, may hold values from -2200 to 2200
- queries: bfloat16 [384, 12, 256], P('ex'), may hold values from -6 to 6
- basis: bfloat16 [12, 256, 256], replicated, may hold values from -0.5 to 2.5
Outputs:
- scores: float32 [384, 16384], P(None, ('slab', 'ex')), parts along dimension 1
The draws below stay inside these ranges and needn't reach their ends.
There are 2 independent parts, one for each index of `slab`. The reference program is written for one: setup_inputs(seed, part) draws one part's arguments, and reference() takes and returns one part's arrays. A program takes and returns all parts, laid end to end along the dimension named above; an argument that names none is the same for every part. Nothing has to cross between parts.
All inputs are finite; a program needn't handle non-finite values.
Results may differ from the reference program's by a relative error of at most 0.0042.
Values may be sent and summed in bfloat16 or wider, within the bound.
A program may use at most 128 MiB of HBM per device.

```python
import math
import jax
import jax.numpy as jnp

R = 256
L = 12
NEX = 8192
NQ = 384


def draw_train_grads(key, part):
    key = jax.random.fold_in(key, 11)
    k_rows, k_noise, k_cols = jax.random.split(key, 3)
    positions = jnp.arange(NEX, dtype=jnp.float32)
    ramp = 1.0 + 2.0 * positions / (NEX - 1)
    row_scale = 10.0 ** jax.random.uniform(k_rows, (NEX,), jnp.float32)
    noise = jnp.clip(jax.random.normal(k_noise, (NEX, L, R), jnp.float32), -4.0, 4.0)
    col_scale = 10.0 ** jax.random.uniform(k_cols, (1, L, R), jnp.float32)
    values = noise * (row_scale * ramp)[:, None, None] * col_scale
    return values.astype(jnp.bfloat16)


def draw_basis(key, part):
    key = jax.random.fold_in(key, 23)
    k_diag, k_off = jax.random.split(key, 2)
    ident = (jnp.arange(R)[:, None] == jnp.arange(R)[None, :]).astype(jnp.float32)
    diag_vals = 1.0 + jax.random.uniform(k_diag, (L, 1, R), jnp.float32)
    off_vals = jnp.clip(jax.random.normal(k_off, (L, R, R), jnp.float32), -4.0, 4.0) * (0.45 / math.sqrt(R))
    return (ident[None, :, :] * diag_vals + off_vals).astype(jnp.bfloat16)


def levels(rng, dims, pieces, least, largest):
    gain, own = 1.0, jax.random.fold_in(rng, 6)
    for axis_at, parts in pieces:
        heights = jnp.exp(jax.random.uniform(jax.random.fold_in(own, axis_at), (parts,), jnp.float32, least / len(pieces), largest / len(pieces)))
        gain = gain * jnp.repeat(heights, dims[axis_at] // parts).reshape([-1 if axis == axis_at else 1 for axis in range(len(dims))])
    return gain


def normal_values(key, extent, deviation, reach, shards=(), kind=jnp.bfloat16):
    values = jax.random.normal(key, extent, jnp.float32) * deviation
    if len(shards) > 0:
        values = levels(key, extent, shards, -0.22, 0.18) * values
    return jnp.clip(values, min=-reach, max=reach).astype(kind)


def setup_inputs(seed: int = 0, part: int = 0) -> dict:
    key_of = jax.random.split(jax.random.key(seed), 4)
    own_keys = jax.random.split(jax.random.fold_in(key_of[3], part), 4)
    return {
        "train_grads": draw_train_grads(jax.random.fold_in(jax.random.fold_in(key_of[3], part), 71), part),
        "queries": normal_values(key_of[1], (NQ, L, R), 1.0, 6.0, ((0, 16),)),
        "basis": draw_basis(jax.random.fold_in(key_of[3], 71), part),
    }


def reference(train_grads, queries, basis):
    sq_rows = []
    for layer_idx in range(L):
        rotated = jnp.dot(train_grads[:, layer_idx, :], basis[layer_idx], preferred_element_type=jnp.float32)
        sq_rows.append(jnp.sum(rotated * rotated, axis=0))
    eigvals = jnp.stack(sq_rows) / NEX
    damped = eigvals + 0.1 * jnp.mean(eigvals, axis=1, keepdims=True)
    pre_rows = []
    for layer_idx in range(L):
        qrot = jnp.dot(queries[:, layer_idx, :], basis[layer_idx], preferred_element_type=jnp.float32)
        scaled = (qrot / damped[layer_idx]).astype(jnp.bfloat16)
        pre_rows.append(jnp.dot(scaled, basis[layer_idx].T, preferred_element_type=jnp.float32).astype(jnp.bfloat16))
    precond = jnp.stack(pre_rows, axis=1)
    return jnp.dot(precond.reshape(NQ, L * R), train_grads.reshape(NEX, L * R).T, preferred_element_type=jnp.float32)
```

```python
import functools
import math

import jax
import jax.numpy as jnp
from jax import lax
from jax.experimental import pallas as pl
from jax.experimental.pallas import tpu as pltpu
from jax.sharding import PartitionSpec as P

MESH = pl.DeviceIdType.MESH
NT = (((1,), (1,)), ((), ()))


def loop(count, body):
    if count <= 4:
        for i in range(count):
            body(i)
    else:
        pl.loop(0, count)(body)


def kernel(
    A, B, t_hbm, q_hbm, b_hbm, out_hbm,
    tv, bv, rot, g, qall, sq, sq1, sq2, ov,
    t_sem, b_sem, own_sem, out_sem, recv, z_send, y_send, x_send, c_send, s1_send, s2_send, s1_recv, s2_recv,
):
    layers, rows, feature = tv.shape
    half = A * B
    total = 2 * half
    blk = ov.shape[1]
    part = layers // 4
    s = lax.axis_index("slab")
    e = lax.axis_index("ex")
    c = lax.rem(e, 2)
    ab = lax.div(e, 2)
    a = lax.div(ab, B)
    b = lax.rem(ab, B)

    def ex_of(a_, b_, c_):
        return (a_ * B + b_) * 2 + c_

    def at(a_, b_, c_, p):
        return (c_ * half + a_ * B + b_) * 4 + p

    def t_copy(l):
        return pltpu.make_async_copy(t_hbm.at[l], tv.at[l], t_sem.at[l])

    def b_copy(l):
        return pltpu.make_async_copy(b_hbm.at[l], bv.at[l], b_sem.at[l])

    for l in range(layers):
        t_copy(l).start()
        b_copy(l).start()
    own = pltpu.make_async_copy(q_hbm, qall.at[pl.ds(at(a, b, c, 0), 4)], own_sem)
    own.start()

    barrier = pltpu.get_barrier_semaphore()

    def greet(device):
        pl.semaphore_signal(barrier, inc=1, device_id=device, device_id_type=MESH)

    loop(A - 1, lambda i: greet((s, ex_of(lax.rem(a + 1 + i, A), b, c))))
    loop(B - 1, lambda i: greet((s, ex_of(a, lax.rem(b + 1 + i, B), c))))
    loop(B, lambda i: greet((s, ex_of(a, lax.rem(b + i, B), 1 - c))))
    greet((1 - s, e))
    pl.semaphore_wait(barrier, A - 1 + 2 * B - 1 + 1)

    def send(src, idx, send_sem, device):
        pltpu.make_async_remote_copy(
            src_ref=src, dst_ref=qall.at[idx], send_sem=send_sem, recv_sem=recv.at[idx],
            device_id=device, device_id_type=MESH,
        ).start()

    def arrived(idx):
        pltpu.make_async_copy(qall.at[idx], qall.at[idx], recv.at[idx]).wait()

    def to_y(src, idx):
        loop(B - 1, lambda i: send(src, idx, y_send, (s, ex_of(a, lax.rem(b + 1 + i, B), c))))

    def to_x(src, idx):
        send(src, idx, x_send, (1 - s, e))

    def to_core(src, idx):
        send(src, idx, c_send, (s, ex_of(a, b, 1 - c)))

    mine = 2 * s
    theirs = 2 - 2 * s

    def send_line(i):
        peer = (s, ex_of(lax.rem(a + 1 + i, A), b, c))
        for t in range(2):
            send(q_hbm.at[mine + t], at(a, b, c, mine + t), z_send, peer)

    loop(A - 1, send_line)
    for p in (mine + 1, mine, theirs):
        to_y(q_hbm.at[p], at(a, b, c, p))
    for p in range(4):
        to_core(q_hbm.at[p], at(a, b, c, p))

    def rotate(l):
        t_copy(l).wait()
        b_copy(l).wait()
        r = jnp.dot(tv[l], bv[l], preferred_element_type=jnp.float32)
        rot[l] = r
        sq[pl.ds(l, 1), :] = jnp.sum(r * r, axis=0, keepdims=True)

    def near(i):
        b_ = lax.rem(b + 1 + i, B)
        idx = at(a, b_, c, mine + 1)
        arrived(idx)
        to_x(qall.at[idx], idx)
        to_core(qall.at[idx], idx)
        for p in (mine, theirs):
            idx = at(a, b_, c, p)
            arrived(idx)
            to_core(qall.at[idx], idx)

    def line(i):
        a_ = lax.rem(a + 1 + i, A)
        for t in (1, 0):
            idx = at(a_, b, c, mine + t)
            arrived(idx)
            to_y(qall.at[idx], idx)
            to_x(qall.at[idx], idx)
            to_core(qall.at[idx], idx)

    def across(i):
        a_ = lax.rem(a + 1 + i, A)
        idx = at(a_, b, c, theirs)
        arrived(idx)
        to_y(qall.at[idx], idx)
        to_core(qall.at[idx], idx)
        idx = at(a_, b, c, theirs + 1)
        arrived(idx)
        to_core(qall.at[idx], idx)

    def far_y(i):
        a_ = lax.rem(a + 1 + i, A)

        def one(j):
            b_ = lax.rem(b + 1 + j, B)
            idx = at(a_, b_, c, mine + 1)
            arrived(idx)
            to_x(qall.at[idx], idx)
            to_core(qall.at[idx], idx)
            idx = at(a_, b_, c, mine)
            arrived(idx)
            to_core(qall.at[idx], idx)

        loop(B - 1, one)

    def far_yy(i):
        a_ = lax.rem(a + 1 + i, A)

        def one(j):
            idx = at(a_, lax.rem(b + 1 + j, B), c, theirs)
            arrived(idx)
            to_core(qall.at[idx], idx)

        loop(B - 1, one)

    def far_x(i):
        a_ = lax.rem(a + i, A)

        def one(j):
            idx = at(a_, lax.rem(b + 1 + j, B), c, theirs + 1)
            arrived(idx)
            to_core(qall.at[idx], idx)

        loop(B - 1, one)

    def sq1_copy(b_, c_):
        slot = b * 2 + c
        return pltpu.make_async_remote_copy(
            src_ref=sq, dst_ref=sq1.at[slot], send_sem=s1_send, recv_sem=s1_recv.at[slot],
            device_id=(s, ex_of(a, b_, c_)), device_id_type=MESH,
        )

    def sq2_copy(a_):
        return pltpu.make_async_remote_copy(
            src_ref=sq2.at[a], dst_ref=sq2.at[a], send_sem=s2_send, recv_sem=s2_recv.at[a],
            device_id=(s, ex_of(a_, b, c)), device_id_type=MESH,
        )

    for l in range(layers):
        rotate(l)
        if l == layers // 2:
            loop(B - 1, near)
    sq1[b * 2 + c] = sq[...]
    loop(B - 1, lambda i: sq1_copy(lax.rem(b + 1 + i, B), c).start())
    loop(B, lambda i: sq1_copy(lax.rem(b + i, B), 1 - c).start())

    line(0)

    def sq1_arrived(b_, c_):
        slot = b_ * 2 + c_
        pltpu.make_async_copy(sq1.at[slot], sq1.at[slot], s1_recv.at[slot]).wait()

    loop(B - 1, lambda i: sq1_arrived(lax.rem(b + 1 + i, B), c))
    loop(B, lambda i: sq1_arrived(lax.rem(b + i, B), 1 - c))
    acc = sq1[0]
    for i in range(1, 2 * B):
        acc = acc + sq1[i]
    sq2[a] = acc
    loop(A - 1, lambda i: sq2_copy(lax.rem(a + 1 + i, A)).start())

    loop(A - 2, lambda i: line(i + 1))
    loop(A - 1, across)

    def sq2_arrived(i):
        slot = lax.rem(a + 1 + i, A)
        pltpu.make_async_copy(sq2.at[slot], sq2.at[slot], s2_recv.at[slot]).wait()

    loop(A - 1, sq2_arrived)
    acc = sq2[0]
    for i in range(1, A):
        acc = acc + sq2[i]
    eig = acc / (rows * total)
    damped = eig + 0.1 * jnp.mean(eig, axis=1, keepdims=True)
    inv = 1.0 / damped

    def project(l):
        scaled = (rot[l] * inv[l : l + 1, :]).astype(jnp.bfloat16)
        g[:, l * feature : (l + 1) * feature] = lax.dot_general(
            scaled, bv[l], NT, preferred_element_type=jnp.float32
        ).astype(jnp.bfloat16)

    for l in range(0, layers // 3):
        project(l)
    loop(A - 1, far_y)
    for l in range(layers // 3, 2 * layers // 3):
        project(l)
    loop(A - 1, far_yy)
    for l in range(2 * layers // 3, layers):
        project(l)
    loop(A, far_x)
    own.wait()

    group = math.gcd(half, 8)
    chunks = half // group

    def score(first):
        cols = []
        for p in range(4):
            for j in range(part):
                cols.append(
                    jnp.concatenate(
                        [qall[(first + i) * 4 + p, j].astype(jnp.float32) for i in range(group)], axis=0
                    ).astype(jnp.bfloat16)
                )
        q = jnp.concatenate(cols, axis=1)
        r = lax.dot_general(q, g[...], NT, preferred_element_type=jnp.float32)
        return r.reshape(group, blk, rows)

    def out_copy(c_, k):
        return pltpu.make_async_copy(
            ov.at[pl.ds(c_ * half + k * group, group)],
            out_hbm.at[pl.ds(k * group, group), c_],
            out_sem.at[c_, k],
        )

    def do_chunk(c_, k):
        first = c_ * half + k * group
        ov[pl.ds(first, group)] = score(first)
        out_copy(c_, k).start()

    loop(chunks, lambda k: do_chunk(c, k))

    def mate(i):
        for p in range(4):
            arrived(((1 - c) * half + i) * 4 + p)

    pl.loop(0, half)(mate)
    loop(chunks, lambda k: do_chunk(1 - c, k))

    def drain(count, sem):
        pltpu.make_async_copy(qall.at[pl.ds(0, count)], qall.at[pl.ds(0, count)], sem).wait()

    drain(2 * (A - 1), z_send)
    drain(3 * A * (B - 1), y_send)
    drain(2 * (A - 1) + A * (B - 1), x_send)
    drain(4 * half, c_send)
    pltpu.make_async_copy(sq1.at[pl.ds(0, 2 * B - 1)], sq1.at[pl.ds(0, 2 * B - 1)], s1_send).wait()
    pltpu.make_async_copy(sq2.at[pl.ds(0, A - 1)], sq2.at[pl.ds(0, A - 1)], s2_send).wait()
    for c_ in range(2):
        loop(chunks, lambda k: out_copy(c_, k).wait())


def local(n, train_grads, queries, basis):
    rows, layers, feature = train_grads.shape
    blk = queries.shape[0]
    half = n // 2
    A = 2 ** ((half.bit_length()) // 2)
    B = half // A
    t = train_grads.transpose(1, 0, 2)
    q = queries.transpose(1, 0, 2).reshape(4, layers // 4, blk, feature)
    group = math.gcd(half, 8)
    dma = pltpu.SemaphoreType.DMA
    anyspec = pl.BlockSpec(memory_space=pl.ANY)
    out = pl.pallas_call(
        functools.partial(kernel, A, B),
        out_shape=jax.ShapeDtypeStruct((half, 2, blk, rows), jnp.float32),
        in_specs=[anyspec] * 3,
        out_specs=anyspec,
        scratch_shapes=[
            pltpu.VMEM((layers, rows, feature), jnp.bfloat16),
            pltpu.VMEM((layers, feature, feature), jnp.bfloat16),
            pltpu.VMEM((layers, rows, feature), jnp.float32),
            pltpu.VMEM((rows, layers * feature), jnp.bfloat16),
            pltpu.VMEM((n * 4, layers // 4, blk, feature), jnp.bfloat16),
            pltpu.VMEM((layers, feature), jnp.float32),
            pltpu.VMEM((2 * B, layers, feature), jnp.float32),
            pltpu.VMEM((A, layers, feature), jnp.float32),
            pltpu.VMEM((n, blk, rows), jnp.float32),
            dma((layers,)),
            dma((layers,)),
            dma,
            dma((2, half // group)),
            dma((n * 4,)),
            dma, dma, dma, dma, dma, dma,
            dma((2 * B,)),
            dma((A,)),
        ],
        compiler_params=pltpu.CompilerParams(
            collective_id=0, has_side_effects=True, vmem_limit_bytes=56 * 1024 * 1024
        ),
        cost_estimate=pl.CostEstimate(
            flops=4 * layers * rows * feature * feature + 2 * n * blk * rows * layers * feature,
            bytes_accessed=2 * layers * feature * (rows + feature + blk) + 4 * n * blk * rows,
            transcendentals=0,
        ),
    )(t, q, basis)
    return out.reshape(n * blk, rows)


def solution(mesh):
    placed = (P(("slab", "ex"), None, None), P("ex", None, None), P())
    return jax.shard_map(
        functools.partial(local, mesh.shape["ex"]), mesh=mesh, in_specs=placed,
        out_specs=P(None, ("slab", "ex")), check_vma=False,
    )
```

```python
import functools
import math

import jax
import jax.numpy as jnp
from jax import lax
from jax.experimental import pallas as pl
from jax.experimental.pallas import tpu as pltpu
from jax.sharding import PartitionSpec as P

VMEM_BYTES = 53 * 1024 * 1024
MESH = pl.DeviceIdType.MESH
NT = (((1,), (1,)), ((), ()))


def loop(count, body):
    if count <= 4:
        for i in range(count):
            body(i)
    else:
        pl.loop(0, count)(body)


def kernel(
    A, B, t_hbm, q_hbm, b_hbm, out_ref,
    tv, bv, rot, g, qall, sq, sq1, sq2,
    t_sem, b_sem, own_sem, recv, z_send, y_send, x_send, c_send, s1_send, s2_send, s1_recv, s2_recv,
):
    layers, rows, feature = tv.shape
    half = A * B
    total = 2 * half
    blk = qall.shape[2]
    part = layers // 4
    s = lax.axis_index("slab")
    e = lax.axis_index("ex")
    c = lax.rem(e, 2)
    ab = lax.div(e, 2)
    a = lax.div(ab, B)
    b = lax.rem(ab, B)

    def ex_of(a_, b_, c_):
        return (a_ * B + b_) * 2 + c_

    def at(a_, b_, c_, p):
        return (c_ * half + a_ * B + b_) * 4 + p

    def t_copy(l):
        return pltpu.make_async_copy(t_hbm.at[l], tv.at[l], t_sem.at[l])

    def b_copy(l):
        return pltpu.make_async_copy(b_hbm.at[l], bv.at[l], b_sem.at[l])

    for l in range(layers):
        t_copy(l).start()
        b_copy(l).start()
    own = pltpu.make_async_copy(q_hbm, qall.at[pl.ds(at(a, b, c, 0), 4)], own_sem)
    own.start()

    barrier = pltpu.get_barrier_semaphore()

    def greet(device):
        pl.semaphore_signal(barrier, inc=1, device_id=device, device_id_type=MESH)

    loop(A - 1, lambda i: greet((s, ex_of(lax.rem(a + 1 + i, A), b, c))))
    loop(B - 1, lambda i: greet((s, ex_of(a, lax.rem(b + 1 + i, B), c))))
    loop(B, lambda i: greet((s, ex_of(a, lax.rem(b + i, B), 1 - c))))
    greet((1 - s, e))
    def rotate(l):
        t_copy(l).wait()
        b_copy(l).wait()
        r = jnp.dot(tv[l], bv[l], preferred_element_type=jnp.float32)
        rot[l] = r
        sq[pl.ds(l, 1), :] = jnp.sum(r * r, axis=0, keepdims=True)

    for l in range(layers // 2):
        rotate(l)
    pl.semaphore_wait(barrier, A - 1 + 2 * B - 1 + 1)

    def send(src, idx, send_sem, device):
        pltpu.make_async_remote_copy(
            src_ref=src, dst_ref=qall.at[idx], send_sem=send_sem, recv_sem=recv.at[idx],
            device_id=device, device_id_type=MESH,
        ).start()

    def arrived(idx):
        pltpu.make_async_copy(qall.at[idx], qall.at[idx], recv.at[idx]).wait()

    def to_y(src, idx):
        loop(B - 1, lambda i: send(src, idx, y_send, (s, ex_of(a, lax.rem(b + 1 + i, B), c))))

    def to_x(src, idx):
        send(src, idx, x_send, (1 - s, e))

    def to_core(src, idx):
        send(src, idx, c_send, (s, ex_of(a, b, 1 - c)))

    mine = 2 * s
    theirs = 2 - 2 * s

    def others(k, body):
        for ahead, there in ((1, a >= k), (-1, a < A - k)):

            @pl.when(there)
            def _():
                body(a - ahead * k)

    def send_line(a_):
        for t in (1, 0):
            send(q_hbm.at[mine + t], at(a, b, c, mine + t), z_send, (s, ex_of(a_, b, c)))

    others(1, send_line)
    for p in (mine + 1, mine, theirs):
        to_y(q_hbm.at[p], at(a, b, c, p))
    for k in range(2, A):
        others(k, send_line)
    for p in range(4):
        to_core(q_hbm.at[p], at(a, b, c, p))

    def near(i):
        b_ = lax.rem(b + 1 + i, B)
        idx = at(a, b_, c, mine + 1)
        arrived(idx)
        to_x(qall.at[idx], idx)
        to_core(qall.at[idx], idx)
        for p in (mine, theirs):
            idx = at(a, b_, c, p)
            arrived(idx)
            to_core(qall.at[idx], idx)

    def line(k):
        def one(a_):
            for t in (1, 0):
                idx = at(a_, b, c, mine + t)
                arrived(idx)

                if t == 1:
                    to_y(qall.at[idx], idx)
                    to_x(qall.at[idx], idx)
                else:
                    to_x(qall.at[idx], idx)
                    to_y(qall.at[idx], idx)
                to_core(qall.at[idx], idx)

        others(k, one)

    def across(k):
        def one(a_):
            idx = at(a_, b, c, theirs)
            arrived(idx)
            to_y(qall.at[idx], idx)
            to_core(qall.at[idx], idx)

        others(k, one)

    def columns(body):
        loop(B - 1, lambda j: body(lax.rem(b + 1 + j, B)))

    def far_y(k):
        def one(a_):
            def col(b_):
                idx = at(a_, b_, c, mine + 1)
                arrived(idx)
                to_x(qall.at[idx], idx)
                to_core(qall.at[idx], idx)

            columns(col)

        others(k, one)

    def last(idx):
        arrived(idx)
        to_core(qall.at[idx], idx)

    def rest(k):
        def one(a_):
            last(at(a_, b, c, theirs + 1))
            columns(lambda b_: last(at(a_, b_, c, mine)))

        others(k, one)

    def rest_far(k):
        def one(a_):
            columns(lambda b_: last(at(a_, b_, c, theirs)))
            columns(lambda b_: last(at(a_, b_, c, theirs + 1)))

        others(k, one)

    def sq1_copy(b_, c_):
        slot = b * 2 + c
        return pltpu.make_async_remote_copy(
            src_ref=sq, dst_ref=sq1.at[slot], send_sem=s1_send, recv_sem=s1_recv.at[slot],
            device_id=(s, ex_of(a, b_, c_)), device_id_type=MESH,
        )

    def sq2_copy(a_):
        return pltpu.make_async_remote_copy(
            src_ref=sq2.at[a], dst_ref=sq2.at[a], send_sem=s2_send, recv_sem=s2_recv.at[a],
            device_id=(s, ex_of(a_, b, c)), device_id_type=MESH,
        )

    for l in range(layers // 2, layers):
        rotate(l)
    sq1[b * 2 + c] = sq[...]
    loop(B - 1, lambda i: sq1_copy(lax.rem(b + 1 + i, B), c).start())
    loop(B, lambda i: sq1_copy(lax.rem(b + i, B), 1 - c).start())

    loop(B - 1, near)
    line(1)

    def sq1_arrived(b_, c_):
        slot = b_ * 2 + c_
        pltpu.make_async_copy(sq1.at[slot], sq1.at[slot], s1_recv.at[slot]).wait()

    loop(B - 1, lambda i: sq1_arrived(lax.rem(b + 1 + i, B), c))
    loop(B, lambda i: sq1_arrived(lax.rem(b + i, B), 1 - c))
    acc = sq1[0]
    for i in range(1, 2 * B):
        acc = acc + sq1[i]
    sq2[a] = acc
    loop(A - 1, lambda i: sq2_copy(lax.rem(a + 1 + i, A)).start())

    for k in range(2, A):
        line(k)
        if k > 2:
            across(k - 2)
            far_y(k - 2)
    for k in range(max(A - 2, 1), A):
        across(k)
        far_y(k)

    def sq2_arrived(i):
        slot = lax.rem(a + 1 + i, A)
        pltpu.make_async_copy(sq2.at[slot], sq2.at[slot], s2_recv.at[slot]).wait()

    loop(A - 1, sq2_arrived)
    acc = sq2[0]
    for i in range(1, A):
        acc = acc + sq2[i]
    eig = acc / (rows * total)
    damped = eig + 0.1 * jnp.mean(eig, axis=1, keepdims=True)
    inv = 1.0 / damped

    def project(l):
        scaled = (rot[l] * inv[l : l + 1, :]).astype(jnp.bfloat16)
        g[:, l * feature : (l + 1) * feature] = lax.dot_general(
            scaled, bv[l], NT, preferred_element_type=jnp.float32
        ).astype(jnp.bfloat16)

    for l in range(0, layers // 2):
        project(l)
    for k in range(1, A):
        rest(k)
    for l in range(layers // 2, layers):
        project(l)
    columns(lambda b_: last(at(a, b_, c, theirs + 1)))
    for k in range(1, A):
        rest_far(k)
    own.wait()

    group = math.gcd(half, 8)
    chunks = half // group

    def score(first):
        cols = []
        for p in range(4):
            for j in range(part):
                cols.append(
                    jnp.concatenate(
                        [qall[(first + i) * 4 + p, j].astype(jnp.float32) for i in range(group)], axis=0
                    ).astype(jnp.bfloat16)
                )
        q = jnp.concatenate(cols, axis=1)
        r = lax.dot_general(q, g[...], NT, preferred_element_type=jnp.float32)
        return r.reshape(group, blk, rows)

    def do_chunk(c_, k):
        r = score(c_ * half + k * group)
        out_ref[pl.ds(k * group, group), pl.ds(c_, 1)] = r.reshape(group, 1, blk, rows)

    loop(chunks, lambda k: do_chunk(c, k))

    def mate(i):
        for p in range(4):
            arrived(((1 - c) * half + i) * 4 + p)

    pl.loop(0, half)(mate)
    loop(chunks, lambda k: do_chunk(1 - c, k))

    def drain(count, sem):
        pltpu.make_async_copy(qall.at[pl.ds(0, count)], qall.at[pl.ds(0, count)], sem).wait()

    drain(2 * (A - 1), z_send)
    drain(3 * A * (B - 1), y_send)
    drain(2 * (A - 1) + A * (B - 1), x_send)
    drain(4 * half, c_send)
    pltpu.make_async_copy(sq1.at[pl.ds(0, 2 * B - 1)], sq1.at[pl.ds(0, 2 * B - 1)], s1_send).wait()
    pltpu.make_async_copy(sq2.at[pl.ds(0, A - 1)], sq2.at[pl.ds(0, A - 1)], s2_send).wait()


def local(n, train_grads, queries, basis):
    rows, layers, feature = train_grads.shape
    blk = queries.shape[0]
    half = n // 2
    A = 2 ** ((half.bit_length()) // 2)
    B = half // A
    t = train_grads.transpose(1, 0, 2)
    q = queries.transpose(1, 0, 2).reshape(4, layers // 4, blk, feature)
    dma = pltpu.SemaphoreType.DMA
    anyspec = pl.BlockSpec(memory_space=pl.ANY)
    out = pl.pallas_call(
        functools.partial(kernel, A, B),
        out_shape=jax.ShapeDtypeStruct((half, 2, blk, rows), jnp.float32),
        in_specs=[anyspec] * 3,
        out_specs=pl.BlockSpec(memory_space=pltpu.VMEM),
        scratch_shapes=[
            pltpu.VMEM((layers, rows, feature), jnp.bfloat16),
            pltpu.VMEM((layers, feature, feature), jnp.bfloat16),
            pltpu.VMEM((layers, rows, feature), jnp.float32),
            pltpu.VMEM((rows, layers * feature), jnp.bfloat16),
            pltpu.VMEM((n * 4, layers // 4, blk, feature), jnp.bfloat16),
            pltpu.VMEM((layers, feature), jnp.float32),
            pltpu.VMEM((2 * B, layers, feature), jnp.float32),
            pltpu.VMEM((A, layers, feature), jnp.float32),
            dma((layers,)),
            dma((layers,)),
            dma,
            dma((n * 4,)),
            dma, dma, dma, dma, dma, dma,
            dma((2 * B,)),
            dma((A,)),
        ],
        compiler_params=pltpu.CompilerParams(
            collective_id=0, has_side_effects=True, vmem_limit_bytes=VMEM_BYTES
        ),
        cost_estimate=pl.CostEstimate(
            flops=4 * layers * rows * feature * feature + 2 * n * blk * rows * layers * feature,
            bytes_accessed=2 * layers * feature * (rows + feature + blk) + 4 * n * blk * rows,
            transcendentals=0,
        ),
    )(t, q, basis)
    return out.reshape(n * blk, rows)


def solution(mesh):
    placed = (P(("slab", "ex"), None, None), P("ex", None, None), P())
    return jax.shard_map(
        functools.partial(local, mesh.shape["ex"]), mesh=mesh, in_specs=placed,
        out_specs=P(None, ("slab", "ex")), check_vma=False,
    )
```

```python
import functools
import math

import jax
import jax.numpy as jnp
from jax import lax
from jax.experimental import pallas as pl
from jax.experimental.pallas import tpu as pltpu
from jax.sharding import PartitionSpec as P

VMEM_BYTES = 53 * 1024 * 1024
MESH = pl.DeviceIdType.MESH
NT = (((1,), (1,)), ((), ()))


def loop(count, body):
    if count <= 4:
        for i in range(count):
            body(i)
    else:
        pl.loop(0, count)(body)


def kernel(
    A, B, t_hbm, q_hbm, b_hbm, out_ref,
    tv, bv, rot, g, qall, sq, sq1, sq2,
    t_sem, b_sem, own_sem, recv, z_send, y_send, x_send, c_send, s1_send, s2_send, s1_recv, s2_recv,
):
    layers, rows, feature = tv.shape
    half = A * B
    total = 2 * half
    blk = qall.shape[2]
    part = layers // 4
    s = lax.axis_index("slab")
    e = lax.axis_index("ex")
    c = lax.rem(e, 2)
    ab = lax.div(e, 2)
    a = lax.div(ab, B)
    b = lax.rem(ab, B)

    def ex_of(a_, b_, c_):
        return (a_ * B + b_) * 2 + c_

    def at(a_, b_, c_, p):
        return (c_ * half + a_ * B + b_) * 4 + p

    def t_copy(l):
        return pltpu.make_async_copy(t_hbm.at[l], tv.at[l], t_sem.at[l])

    def b_copy(l):
        return pltpu.make_async_copy(b_hbm.at[l], bv.at[l], b_sem.at[l])

    for l in range(layers):
        t_copy(l).start()
        b_copy(l).start()
    own = pltpu.make_async_copy(q_hbm, qall.at[pl.ds(at(a, b, c, 0), 4)], own_sem)
    own.start()

    barrier = pltpu.get_barrier_semaphore()

    def greet(device):
        pl.semaphore_signal(barrier, inc=1, device_id=device, device_id_type=MESH)

    loop(A - 1, lambda i: greet((s, ex_of(lax.rem(a + 1 + i, A), b, c))))
    loop(B - 1, lambda i: greet((s, ex_of(a, lax.rem(b + 1 + i, B), c))))
    loop(B, lambda i: greet((s, ex_of(a, lax.rem(b + i, B), 1 - c))))
    greet((1 - s, e))
    def rotate(l):
        t_copy(l).wait()
        b_copy(l).wait()
        r = jnp.dot(tv[l], bv[l], preferred_element_type=jnp.float32)
        rot[l] = r
        sq[pl.ds(l, 1), :] = jnp.sum(r * r, axis=0, keepdims=True)

    for l in range(layers // 2):
        rotate(l)
    pl.semaphore_wait(barrier, A - 1 + 2 * B - 1 + 1)

    def send(src, idx, send_sem, device):
        pltpu.make_async_remote_copy(
            src_ref=src, dst_ref=qall.at[idx], send_sem=send_sem, recv_sem=recv.at[idx],
            device_id=device, device_id_type=MESH,
        ).start()

    def arrived(idx):
        pltpu.make_async_copy(qall.at[idx], qall.at[idx], recv.at[idx]).wait()

    def to_y(src, idx):
        loop(B - 1, lambda i: send(src, idx, y_send, (s, ex_of(a, lax.rem(b + 1 + i, B), c))))

    def to_x(src, idx):
        send(src, idx, x_send, (1 - s, e))

    def to_core(src, idx):
        send(src, idx, c_send, (s, ex_of(a, b, 1 - c)))

    mine = 2 * s
    theirs = 2 - 2 * s

    def others(k, body):
        for ahead, there in ((1, a >= k), (-1, a < A - k)):

            @pl.when(there)
            def _():
                body(a - ahead * k)

    def send_line(a_):
        for t in (1, 0):
            send(q_hbm.at[mine + t], at(a, b, c, mine + t), z_send, (s, ex_of(a_, b, c)))

    others(1, send_line)
    for p in (mine + 1, mine, theirs):
        to_y(q_hbm.at[p], at(a, b, c, p))
    for k in range(2, A):
        others(k, send_line)
    for p in range(4):
        to_core(q_hbm.at[p], at(a, b, c, p))

    def near(i):
        b_ = lax.rem(b + 1 + i, B)
        idx = at(a, b_, c, mine + 1)
        arrived(idx)
        to_x(qall.at[idx], idx)
        to_core(qall.at[idx], idx)
        for p in (mine, theirs):
            idx = at(a, b_, c, p)
            arrived(idx)
            to_core(qall.at[idx], idx)

    def line(k):
        def one(a_):
            for t in (1, 0):
                idx = at(a_, b, c, mine + t)
                arrived(idx)

                if t == 1:
                    to_y(qall.at[idx], idx)
                    to_x(qall.at[idx], idx)
                else:
                    to_x(qall.at[idx], idx)
                    to_y(qall.at[idx], idx)
                to_core(qall.at[idx], idx)

        others(k, one)

    def across(k):
        def one(a_):
            idx = at(a_, b, c, theirs)
            arrived(idx)
            to_y(qall.at[idx], idx)
            to_core(qall.at[idx], idx)

        others(k, one)

    def columns(body):
        loop(B - 1, lambda j: body(lax.rem(b + 1 + j, B)))

    def far_y(k):
        def one(a_):
            def col(b_):
                idx = at(a_, b_, c, mine + 1)
                arrived(idx)
                to_x(qall.at[idx], idx)
                to_core(qall.at[idx], idx)

            columns(col)

        others(k, one)

    def last(idx):
        arrived(idx)
        to_core(qall.at[idx], idx)

    def rest(k):
        def one(a_):
            last(at(a_, b, c, theirs + 1))
            columns(lambda b_: last(at(a_, b_, c, mine)))

        others(k, one)

    def rest_far(k):
        def one(a_):
            columns(lambda b_: last(at(a_, b_, c, theirs)))
            columns(lambda b_: last(at(a_, b_, c, theirs + 1)))

        others(k, one)

    def sq1_copy(b_, c_):
        slot = b * 2 + c
        return pltpu.make_async_remote_copy(
            src_ref=sq, dst_ref=sq1.at[slot], send_sem=s1_send, recv_sem=s1_recv.at[slot],
            device_id=(s, ex_of(a, b_, c_)), device_id_type=MESH,
        )

    def sq2_copy(a_):
        return pltpu.make_async_remote_copy(
            src_ref=sq2.at[a], dst_ref=sq2.at[a], send_sem=s2_send, recv_sem=s2_recv.at[a],
            device_id=(s, ex_of(a_, b, c)), device_id_type=MESH,
        )

    for l in range(layers // 2, layers):
        rotate(l)
    sq1[b * 2 + c] = sq[...]
    loop(B - 1, lambda i: sq1_copy(lax.rem(b + 1 + i, B), c).start())
    loop(B, lambda i: sq1_copy(lax.rem(b + i, B), 1 - c).start())

    loop(B - 1, near)
    line(1)

    def sq1_arrived(b_, c_):
        slot = b_ * 2 + c_
        pltpu.make_async_copy(sq1.at[slot], sq1.at[slot], s1_recv.at[slot]).wait()

    loop(B - 1, lambda i: sq1_arrived(lax.rem(b + 1 + i, B), c))
    loop(B, lambda i: sq1_arrived(lax.rem(b + i, B), 1 - c))
    acc = sq1[0]
    for i in range(1, 2 * B):
        acc = acc + sq1[i]
    sq2[a] = acc
    loop(A - 1, lambda i: sq2_copy(lax.rem(a + 1 + i, A)).start())

    for k in range(2, A):
        line(k)
        if k > 2:
            across(k - 2)
            far_y(k - 2)
    for k in range(max(A - 2, 1), A):
        across(k)
        far_y(k)

    def sq2_arrived(i):
        slot = lax.rem(a + 1 + i, A)
        pltpu.make_async_copy(sq2.at[slot], sq2.at[slot], s2_recv.at[slot]).wait()

    loop(A - 1, sq2_arrived)
    acc = sq2[0]
    for i in range(1, A):
        acc = acc + sq2[i]
    eig = acc / (rows * total)
    damped = eig + 0.1 * jnp.mean(eig, axis=1, keepdims=True)
    inv = 1.0 / damped

    def project(l):
        scaled = (rot[l] * inv[l : l + 1, :]).astype(jnp.bfloat16)
        g[:, l * feature : (l + 1) * feature] = lax.dot_general(
            scaled, bv[l], NT, preferred_element_type=jnp.float32
        ).astype(jnp.bfloat16)

    for l in range(0, layers // 2):
        project(l)
    for k in range(1, A):
        rest(k)
    for l in range(layers // 2, layers):
        project(l)
    own.wait()

    group = math.gcd(half, 8)
    chunks = half // group

    depth = 2 * part * feature

    def score(first, h):
        cols = []
        for t in range(2):
            for j in range(part):
                cols.append(
                    jnp.concatenate(
                        [qall[(first + i) * 4 + 2 * h + t, j].astype(jnp.float32) for i in range(group)], axis=0
                    ).astype(jnp.bfloat16)
                )
        q = jnp.concatenate(cols, axis=1)
        gs = g[:, pl.ds(pl.multiple_of(h * depth, depth), depth)]
        return lax.dot_general(q, gs, NT, preferred_element_type=jnp.float32).reshape(group, 1, blk, rows)

    def do_half(c_, h, add):
        def one(k):
            place = (pl.ds(k * group, group), pl.ds(c_, 1))
            r = score(c_ * half + k * group, h)
            out_ref[place] = out_ref[place] + r if add else r

        loop(chunks, one)

    def mate(h):
        def one(i):
            for t in range(2):
                arrived(((1 - c) * half + i) * 4 + 2 * h + t)

        pl.loop(0, half)(one)

    do_half(c, s, False)
    columns(lambda b_: last(at(a, b_, c, theirs + 1)))
    if True:
        mate(s)
        do_half(1 - c, s, False)
    for k in range(1, A):
        rest_far(k)
    do_half(c, 1 - s, True)
    if not True:
        mate(s)
        do_half(1 - c, s, False)
    mate(1 - s)
    do_half(1 - c, 1 - s, True)

    def drain(count, sem):
        pltpu.make_async_copy(qall.at[pl.ds(0, count)], qall.at[pl.ds(0, count)], sem).wait()

    drain(2 * (A - 1), z_send)
    drain(3 * A * (B - 1), y_send)
    drain(2 * (A - 1) + A * (B - 1), x_send)
    drain(4 * half, c_send)
    pltpu.make_async_copy(sq1.at[pl.ds(0, 2 * B - 1)], sq1.at[pl.ds(0, 2 * B - 1)], s1_send).wait()
    pltpu.make_async_copy(sq2.at[pl.ds(0, A - 1)], sq2.at[pl.ds(0, A - 1)], s2_send).wait()


def local(n, train_grads, queries, basis):
    rows, layers, feature = train_grads.shape
    blk = queries.shape[0]
    half = n // 2
    A = 2 ** ((half.bit_length()) // 2)
    B = half // A
    t = train_grads.transpose(1, 0, 2)
    q = queries.transpose(1, 0, 2).reshape(4, layers // 4, blk, feature)
    dma = pltpu.SemaphoreType.DMA
    anyspec = pl.BlockSpec(memory_space=pl.ANY)
    out = pl.pallas_call(
        functools.partial(kernel, A, B),
        out_shape=jax.ShapeDtypeStruct((half, 2, blk, rows), jnp.float32),
        in_specs=[anyspec] * 3,
        out_specs=pl.BlockSpec(memory_space=pltpu.VMEM),
        scratch_shapes=[
            pltpu.VMEM((layers, rows, feature), jnp.bfloat16),
            pltpu.VMEM((layers, feature, feature), jnp.bfloat16),
            pltpu.VMEM((layers, rows, feature), jnp.float32),
            pltpu.VMEM((rows, layers * feature), jnp.bfloat16),
            pltpu.VMEM((n * 4, layers // 4, blk, feature), jnp.bfloat16),
            pltpu.VMEM((layers, feature), jnp.float32),
            pltpu.VMEM((2 * B, layers, feature), jnp.float32),
            pltpu.VMEM((A, layers, feature), jnp.float32),
            dma((layers,)),
            dma((layers,)),
            dma,
            dma((n * 4,)),
            dma, dma, dma, dma, dma, dma,
            dma((2 * B,)),
            dma((A,)),
        ],
        compiler_params=pltpu.CompilerParams(
            collective_id=0, has_side_effects=True, vmem_limit_bytes=VMEM_BYTES
        ),
        cost_estimate=pl.CostEstimate(
            flops=4 * layers * rows * feature * feature + 2 * n * blk * rows * layers * feature,
            bytes_accessed=2 * layers * feature * (rows + feature + blk) + 4 * n * blk * rows,
            transcendentals=0,
        ),
    )(t, q, basis)
    return out.reshape(n * blk, rows)


def solution(mesh):
    placed = (P(("slab", "ex"), None, None), P("ex", None, None), P())
    return jax.shard_map(
        functools.partial(local, mesh.shape["ex"]), mesh=mesh, in_specs=placed,
        out_specs=P(None, ("slab", "ex")), check_vma=False,
    )
```
